768 devices in a mesh: sub: 192 (over y, z, core), own: 4 (over x).
Axes of the slice: x: 4, y: 8, z: 12, core: 2. Of those that a mesh axis runs over, the one named last changes fastest.
Arguments:
- zbasis: bfloat16 [192, 4, 8192, 128], P('sub', 'own'), may hold values from -0.09375 to 0.09375
- stiff: bfloat16 [192, 4, 128, 64, 64], P('sub', 'own')
- ov_index: int32 [192, 4, 2, 512], P('sub', 'own'), may hold values from 0 to 8191
- owner_map: int32 [192, 4, 16, 1], P('sub', 'own'), may hold values from 0 to 3; in each aligned block of 16 rows (0 to 15, 16 to 31, ..., all dimensions but the last counted through in order) at most 8 rows name the same one
- coarse_vec: float32 [192, 4, 128], P('sub', 'own'), may hold values from -6 to 6
Outputs:
- owner_tiles: float32 [192, 4, 4, 8, 8, 384], P('sub', 'own')
- coarse_product: float32 [192, 4, 128], P('sub', 'own')
The draws below stay inside these ranges and needn't reach their ends.
Inputs may be any that keep to these rules, and one draw needn't show every extreme that they name: `owner_map`: among the 16 tiles of one subdomain no owner is named more than 8 times, and some subdomain names some owner exactly 8 times. `ov_index`: each entry is a row of the subdomain's 8192 unknowns; entries may repeat.
All inputs are finite; a program needn't handle non-finite values.
Results may differ from the reference program's by a relative error of at most 0.00044.
Values may be sent and summed in bfloat16 or wider, within the bound.
No kernel may reach another device: no remote copies, remote signals or barrier semaphores. Data moves between devices by JAX's collectives and lax.ppermute only.
A program may use at most 32 MiB of HBM per device.

```python
import math
import jax
import jax.numpy as jnp
import numpy as np
from jax import lax

K = 128
BS = 64
NLOC = 8192
OV = 512
TR = 8
RT = 16
SCAP = 8
NB = 128
SUBS = 192
OWNERS = 4


def draw_stiff(key, part):
    key = jax.random.fold_in(key, 11)
    key_off, key_diag = jax.random.split(key)
    off_part = jax.random.normal(key_off, (SUBS, OWNERS, NB, BS, BS), jnp.float32) * 0.05
    diag_part = jnp.exp(jax.random.uniform(key_diag, (SUBS, OWNERS, NB, BS), jnp.float32, minval=math.log(0.5), maxval=math.log(4.0)))
    identity = jnp.eye(BS, dtype=jnp.float32)
    return (off_part * (1.0 - identity) + diag_part[..., None] * identity).astype(jnp.bfloat16)


def plant(drawn, stream_key, least, largest):
    spot = [jax.random.randint(jax.random.fold_in(stream_key, axis), (), 0, length) for axis, length in enumerate(drawn.shape)]
    main_axis = drawn.shape.index(max(drawn.shape))
    beside = spot[:main_axis] + [(spot[main_axis] + 1) % drawn.shape[main_axis]] + spot[main_axis + 1:]
    return drawn.at[tuple(spot)].set(least).at[tuple(beside)].set(largest)


def block_levels(stream_key, shape, cuts, smallest, largest):
    level, own = 1.0, jax.random.fold_in(stream_key, 6)
    for dim, parts in cuts:
        steps = jnp.exp(jax.random.uniform(jax.random.fold_in(own, dim), (parts,), jnp.float32, smallest / len(cuts), largest / len(cuts)))
        level = level * jnp.repeat(steps, shape[dim] // parts).reshape([-1 if axis == dim else 1 for axis in range(len(shape))])
    return level


def shared_out(stream_key, own, number, rows, amount, top, reach, lean):
    ranking = jax.random.permutation(stream_key, amount)
    heavy_load, ordinary = portions_of(amount, rows * top, reach, lean, True), portions_of(amount, rows * top, reach, lean, False)
    places = jnp.arange(amount)

    def named(sizes, rotation):
        used = int((sizes > 0).sum())
        fixed = max(1, used // 4)
        shifted = fixed + (places - fixed + rotation * (used - fixed)) % max(1, amount - fixed)
        return jnp.zeros((amount,), jnp.int32).at[ranking[jnp.where(places < fixed, places, shifted)]].set(jnp.asarray(sizes, jnp.int32))

    sizes = jnp.where(number % 4 == 0, named(heavy_load, number // 4), named(ordinary, number - number // 4 - 1))
    mixed = jax.random.permutation(jax.random.fold_in(own, 3), amount)
    donor, receiver = mixed[0:amount // 2 * 2:2], mixed[1:amount // 2 * 2:2]
    room = jnp.minimum(sizes[donor] - 1, reach - sizes[receiver]) // 2
    room = jnp.where((donor == ranking[0]) | (receiver == ranking[0]) | (sizes[receiver] == 0), 0, jnp.maximum(room, 0))
    shifted = jax.random.randint(jax.random.fold_in(own, 4), (amount // 2,), 0, 1 << 20) % (room + 1)
    sizes = sizes.at[donor].add(-shifted).at[receiver].add(shifted)
    labels = jnp.searchsorted(jnp.cumsum(sizes), jnp.arange(rows * top), side="right").astype(jnp.int32)
    listing = labels.reshape(top, rows).T
    listing = listing[jax.random.permutation(jax.random.fold_in(own, 1), rows)]
    rotation = jax.random.randint(jax.random.fold_in(own, 2), (rows, 1), 0, top)
    return jnp.take_along_axis(listing, (jnp.arange(top)[None, :] + rotation) % top, axis=1)


def portions_of(amount, total, limit, lean, full):
    portions = [(1 << 20) // math.isqrt(standing ** lean) + 1 for standing in range(1, amount + 1)]
    largest = limit if full else min(limit, max(-(-total // amount), total * portions[0] // sum(portions)))
    least = 1 if total - largest >= amount - 1 else 0
    given, spare = [largest] + [least] * (amount - 1), total - largest - least * (amount - 1)
    while spare > 0:
        candidates = [i for i in range(1, amount) if given[i] < largest] or [i for i in range(1, amount) if given[i] < limit]
        mass, budget = sum([portions[i] for i in candidates]), spare
        for i in candidates:
            addition = min(limit - given[i], max(1, budget * portions[i] // mass), spare)
            given[i] = given[i] + addition
            spare = spare - addition
    return np.array(given)


def noise(own_key, extent, deviation, bound, pieces=(), kind=jnp.bfloat16):
    array = jax.random.normal(own_key, extent, jnp.float32) * deviation
    if len(pieces) > 0:
        array = block_levels(own_key, extent, pieces, -0.22, 0.18) * array
    return jnp.clip(array, min=-bound, max=bound).astype(kind)


def setup_inputs(seed: int = 0) -> dict:
    key_list = jax.random.split(jax.random.key(seed), 6)
    zbasis = noise(key_list[0], (SUBS, OWNERS, NLOC, K), (NLOC // 2) ** -0.5, 0.09375, ((0, 192), (1, 4)))
    stiff = draw_stiff(jax.random.fold_in(key_list[5], 71), 0)
    ov_index = plant(jax.random.randint(key_list[2], (SUBS, OWNERS, 2, OV), 0, NLOC), jax.random.fold_in(key_list[2], 1), 0, NLOC - 1).astype(jnp.int32)
    owner_map_keys = jax.random.split(jax.random.fold_in(key_list[3], 1), SUBS * OWNERS * RT // RT)
    owner_map_turns = jax.random.permutation(jax.random.fold_in(key_list[3], 3), SUBS * OWNERS * RT // RT)
    owner_map = jax.vmap(lambda own, number: shared_out(jax.random.fold_in(key_list[3], 2), own, number, RT, OWNERS, 1, SCAP, 2))(owner_map_keys, owner_map_turns).reshape((SUBS, OWNERS, RT, 1))
    coarse_vec = noise(key_list[4], (SUBS, OWNERS, K), 1.0, 6.0, ((0, 192), (1, 4)), jnp.float32)
    return dict(zbasis=zbasis, stiff=stiff, ov_index=ov_index, owner_map=owner_map, coarse_vec=coarse_vec)


def select_slots(mapping, target, capacity):
    matches = (mapping == target).astype(jnp.int32)
    position = jnp.cumsum(matches, axis=-1) - 1
    slot_ids = jnp.arange(capacity, dtype=jnp.int32)
    chosen = (matches[..., None, :] == 1) & (position[..., None, :] == slot_ids[:, None])
    return chosen.astype(jnp.float32)


def local_rows(items):
    deflation, blocks, margin = items
    count_blocks = blocks.shape[0]
    applied = jnp.einsum('bij,bjk->bik', blocks.astype(jnp.float32),
                         deflation.reshape(count_blocks, BS, K).astype(jnp.float32),
                         precision=lax.Precision.HIGHEST).reshape(NLOC, K).astype(jnp.bfloat16)
    self_block = jnp.einsum('na,nb->ab', deflation.astype(jnp.float32), applied.astype(jnp.float32),
                            precision=lax.Precision.HIGHEST)
    w_first = jnp.take(applied, margin[0], axis=0)
    w_second = jnp.take(applied, margin[1], axis=0)
    z_first = jnp.take(deflation, margin[0], axis=0)
    z_second = jnp.take(deflation, margin[1], axis=0)
    return self_block, w_first, w_second, z_first, z_second


def reference(zbasis, stiff, ov_index, owner_map, coarse_vec):
    total = SUBS * OWNERS
    self_block, w_first, w_second, z_first, z_second = lax.map(
        local_rows,
        (zbasis.reshape(total, NLOC, K), stiff.reshape(total, NB, BS, BS), ov_index.reshape(total, 2, OV)))
    self_block = self_block.reshape(SUBS, OWNERS, K, K)
    w_first = w_first.reshape(SUBS, OWNERS, OV, K)
    w_second = w_second.reshape(SUBS, OWNERS, OV, K)
    z_first = z_first.reshape(SUBS, OWNERS, OV, K)
    z_second = z_second.reshape(SUBS, OWNERS, OV, K)
    from_left = jnp.concatenate([jnp.zeros_like(w_second[:1]), w_second[:-1]], axis=0)
    from_right = jnp.concatenate([w_first[1:], jnp.zeros_like(w_first[:1])], axis=0)
    left_block = jnp.einsum('xyna,xynb->xyab', z_first.astype(jnp.float32), from_left.astype(jnp.float32),
                            precision=lax.Precision.HIGHEST)
    right_block = jnp.einsum('xyna,xynb->xyab', z_second.astype(jnp.float32), from_right.astype(jnp.float32),
                             precision=lax.Precision.HIGHEST)
    vec_left = jnp.concatenate([jnp.zeros_like(coarse_vec[:1]), coarse_vec[:-1]], axis=0)
    vec_right = jnp.concatenate([coarse_vec[1:], jnp.zeros_like(coarse_vec[:1])], axis=0)
    coarse_product = (jnp.einsum('xyab,xyb->xya', left_block, vec_left, precision=lax.Precision.HIGHEST)
                      + jnp.einsum('xyab,xyb->xya', self_block, coarse_vec, precision=lax.Precision.HIGHEST)
                      + jnp.einsum('xyab,xyb->xya', right_block, vec_right, precision=lax.Precision.HIGHEST))
    block_row = jnp.concatenate([left_block, self_block, right_block], axis=-1)
    row_tiles = block_row.reshape(SUBS, OWNERS, RT, TR, 3 * K)
    mapping = owner_map[..., 0]
    targets = jnp.arange(OWNERS, dtype=jnp.int32)[None, None, :, None]
    chosen = select_slots(mapping[:, :, None, :], targets, SCAP)
    owner_tiles = jnp.einsum('xpqst,xptrc->xqpsrc', chosen, row_tiles, precision=lax.Precision.HIGHEST)
    return owner_tiles, coarse_product
```

```python
import functools

import jax
import jax.numpy as jnp
from jax import lax
from jax.experimental import pallas as pl
from jax.experimental.pallas import tpu as pltpu
from jax.sharding import PartitionSpec as P

TR = 8
SCAP = 8
PAD = 16
UNROLL = 8
F32 = jnp.float32
BF16 = jnp.bfloat16
SMEM = pl.BlockSpec(memory_space=pltpu.SMEM)
VMEM = pl.BlockSpec(memory_space=pltpu.VMEM)
ANY = pl.BlockSpec(memory_space=pl.ANY)


def parity():
    return lax.rem(lax.axis_index("sub"), 2)


def split3(x):
    hi = x.astype(BF16)
    rest = x - hi.astype(F32)
    mid = rest.astype(BF16)
    low = (rest - mid.astype(F32)).astype(BF16)
    return jnp.concatenate([hi, mid, low, jnp.zeros((PAD - 3, x.shape[1]), BF16)], axis=0)


def gather_rows(idx, side, source, target, base, count):
    @pl.loop(0, count // UNROLL)
    def _(g):
        first = g * UNROLL
        for r in range(UNROLL):
            row = idx[side, first + r]
            target[pl.ds(base + first + r, 1), :] = source[pl.ds(row, 1), :]


def apply_kernel(idx, z_hbm, a_hbm, vec, cross, inner, applied, z_v, a_v, x_v, w_v, rows_v, sems):
    order, _, nb = a_v.shape
    half = order // 2
    lanes = z_v.shape[1]
    count = idx.shape[1]
    pitch = nb + 8
    copy_a = pltpu.make_async_copy(a_hbm, a_v, sems.at[0])
    copy_z = pltpu.make_async_copy(z_hbm, z_v, sems.at[1])
    copy_a.start()
    copy_z.start()
    extra = split3(vec[...])
    cross[pl.ds(count, PAD), :] = extra
    inner[pl.ds(count, PAD), :] = extra
    copy_a.wait()

    @pl.loop(0, half, unroll=4)
    def _(p):
        pair = jnp.concatenate([a_v[p], a_v[p + half]], axis=0)
        x_v[pl.ds(pl.multiple_of(p * pitch, 8), nb), :] = pair.T.astype(F32)

    copy_z.wait()

    @pl.loop(0, nb, unroll=8)
    def _(b):
        at = pl.multiple_of(b * order, order)
        left = x_v[pl.ds(b, half, stride=pitch), :].astype(BF16)
        zb = z_v[pl.ds(at, order), :]
        zero = jnp.zeros_like(zb)
        right = jnp.concatenate(
            [jnp.concatenate([zb, zero], axis=1), jnp.concatenate([zero, zb], axis=1)], axis=0
        )
        out = jnp.dot(left, right, preferred_element_type=F32)
        out = jnp.concatenate([out[:, :lanes], out[:, lanes:]], axis=0)
        w_v[pl.ds(at, order), :] = out
        applied[pl.ds(at, order), :] = out.astype(BF16)

    mine = parity()
    gather_rows(idx, mine, w_v, rows_v, 0, count)
    cross[pl.ds(0, count), :] = rows_v[pl.ds(0, count), :].astype(BF16)
    gather_rows(idx, 1 - mine, w_v, rows_v, count, count)
    inner[pl.ds(0, count), :] = rows_v[pl.ds(count, count), :].astype(BF16)


def local_kernel(idx, z, applied, self_block, zt, z_f, rows_v):
    n, lanes = z.shape
    count = idx.shape[1]
    step = 512

    self_block[...] = jnp.zeros_like(self_block)

    @pl.loop(0, n // step)
    def _(s):
        at = pl.multiple_of(s * step, step)
        part = z[pl.ds(at, step), :]
        z_f[pl.ds(at, step), :] = part.astype(F32)
        self_block[...] += lax.dot_general(
            part, applied[pl.ds(at, step), :], (((0,), (0,)), ((), ())), preferred_element_type=F32
        )

    mine = parity()
    gather_rows(idx, mine, z_f, rows_v, 0, count)
    gather_rows(idx, 1 - mine, z_f, rows_v, count, count)
    zt[...] = rows_v[...].astype(BF16).T


def pack_kernel(owner, cross, inner, zt, self_block, vec, tiles, product, row_v, used):
    lanes = self_block.shape[0]
    count = zt.shape[1] // 2
    mine = parity()

    def joined(ref):
        extra = ref[pl.ds(count, PAD), :].astype(F32)
        return extra[0:1] + (extra[1:2] + extra[2:3])

    tiles[...] = jnp.zeros_like(tiles)
    by_cross = jnp.dot(zt[:, :count], cross[pl.ds(0, count), :], preferred_element_type=F32)
    by_inner = jnp.dot(zt[:, count:], inner[pl.ds(0, count), :], preferred_element_type=F32)
    own = self_block[...]
    at = pl.multiple_of(mine * (2 * lanes), lanes)
    row_v[:, pl.ds(at, lanes)] = by_cross
    row_v[:, pl.ds(pl.multiple_of(2 * lanes - at, lanes), lanes)] = by_inner
    row_v[:, pl.ds(lanes, lanes)] = own
    total = by_cross * joined(cross) + own * vec[...] + by_inner * joined(inner)
    product[...] = jnp.sum(total.T, axis=0, keepdims=True)
    for q in range(tiles.shape[0]):
        used[q] = 0
    for t in range(owner.shape[1]):
        q = owner[0, t]
        slot = used[q]
        used[q] = slot + 1
        tiles[q, slot] = row_v[pl.ds(t * TR, TR), :]


def per_device(zbasis, stiff, ov_index, owner_map, coarse_vec):
    z = zbasis[0, 0]
    a = jnp.transpose(stiff[0, 0], (1, 2, 0))
    idx = ov_index[0, 0]
    owner = owner_map[0, 0, :, 0].reshape(1, -1)
    vec = coarse_vec[0]
    n, lanes = z.shape
    order, _, nb = a.shape
    count = idx.shape[1]
    chain = lax.axis_size("sub")
    owners = lax.axis_size("own")
    sent = jax.ShapeDtypeStruct((count + PAD, lanes), BF16)
    cross, inner, applied = pl.pallas_call(
        apply_kernel,
        name="apply",
        out_shape=(sent, sent, jax.ShapeDtypeStruct((n, lanes), BF16)),
        in_specs=[SMEM, ANY, ANY, VMEM],
        out_specs=(VMEM, VMEM, VMEM),
        scratch_shapes=[
            pltpu.VMEM((n, lanes), BF16),
            pltpu.VMEM((order, order, nb), BF16),
            pltpu.VMEM((order // 2 * (nb + 8), 2 * order), F32),
            pltpu.VMEM((n, lanes), F32),
            pltpu.VMEM((2 * count, lanes), F32),
            pltpu.SemaphoreType.DMA((2,)),
        ],
        compiler_params=pltpu.CompilerParams(vmem_limit_bytes=40 << 20),
        cost_estimate=pl.CostEstimate(flops=2 * n * order * lanes, bytes_accessed=6 << 20, transcendentals=0),
    )(idx, z, a, vec)
    pairs = [(i, i + 1) for i in range(1, chain - 1, 2)]
    got_cross = lax.ppermute(cross, "sub", pairs + [(j, i) for i, j in pairs])
    got_inner = lax.ppermute(inner, "sub", [(i, i ^ 1) for i in range(chain)])
    self_block, zt = pl.pallas_call(
        local_kernel,
        name="local",
        out_shape=(
            jax.ShapeDtypeStruct((lanes, lanes), F32),
            jax.ShapeDtypeStruct((lanes, 2 * count), BF16),
        ),
        in_specs=[SMEM, VMEM, VMEM],
        out_specs=(VMEM, VMEM),
        scratch_shapes=[pltpu.VMEM((n, lanes), F32), pltpu.VMEM((2 * count, lanes), F32)],
        compiler_params=pltpu.CompilerParams(vmem_limit_bytes=40 << 20),
        cost_estimate=pl.CostEstimate(flops=2 * n * lanes * lanes, bytes_accessed=5 << 20, transcendentals=0),
    )(idx, z, applied)
    tiles, product = pl.pallas_call(
        pack_kernel,
        name="pack",
        out_shape=(
            jax.ShapeDtypeStruct((owners, SCAP, TR, 3 * lanes), F32),
            jax.ShapeDtypeStruct((1, lanes), F32),
        ),
        in_specs=[SMEM, VMEM, VMEM, VMEM, VMEM, VMEM],
        out_specs=(VMEM, VMEM),
        scratch_shapes=[pltpu.VMEM((lanes, 3 * lanes), F32), pltpu.SMEM((owners,), jnp.int32)],
        compiler_params=pltpu.CompilerParams(vmem_limit_bytes=16 << 20),
    )(owner, got_cross, got_inner, zt, self_block, vec)
    received = lax.all_to_all(tiles, "own", 0, 0, tiled=True)
    return received[None, None], product[None]


def solution(mesh):
    in_specs = (
        P("sub", "own", None, None),
        P("sub", "own", None, None, None),
        P("sub", "own", None, None),
        P("sub", "own", None, None),
        P("sub", "own", None),
    )
    out_specs = (P("sub", "own", None, None, None, None), P("sub", "own", None))
    return jax.shard_map(
        per_device, mesh=mesh, in_specs=in_specs, out_specs=out_specs, check_vma=False
    )
```

```python
import jax
import jax.numpy as jnp
from jax import lax
from jax.experimental import pallas as pl
from jax.experimental.pallas import tpu as pltpu
from jax.sharding import PartitionSpec as P

TR = 8
SCAP = 8
PAD = 16
STEP = 512
A_CUTS = 2
Z_CUTS = 4
ROOM = 58 << 20
BASIS_ROOM = 40 << 20
PACK_ROOM = 16 << 20
F32 = jnp.float32
BF16 = jnp.bfloat16
SMEM = pl.BlockSpec(memory_space=pltpu.SMEM)
VMEM = pl.BlockSpec(memory_space=pltpu.VMEM)
HBM = pl.BlockSpec(memory_space=pltpu.HBM)


def parity():
    return lax.rem(lax.axis_index("sub"), 2)


def split3(x):
    hi = x.astype(BF16)
    rest = x - hi.astype(F32)
    mid = rest.astype(BF16)
    low = (rest - mid.astype(F32)).astype(BF16)
    return jnp.concatenate([hi, mid, low, jnp.zeros((PAD - 3, x.shape[1]), BF16)], axis=0)


def gather_rows(idx, side, source, target):
    for r in range(idx.shape[1]):
        target[pl.ds(r, 1), :] = source[pl.ds(idx[side, r], 1), :]


def apply_kernel(
    idx_hbm, z_hbm, a_hbm, vec, cross, inner, self_block, idx, z_v, a_v, x_v, w_v, rows_v, sent, self_v, sems
):
    order, _, nb = a_v.shape
    half = order // 2
    n, lanes = z_v.shape
    count = idx.shape[1]
    pitch = nb + 8
    quarter = half // A_CUTS
    slab = n // Z_CUTS
    copy_idx = pltpu.make_async_copy(idx_hbm, idx, sems.at[0])
    copy_idx.start()
    copies_a, copies_z = [], []
    for c in range(A_CUTS):
        for h in range(2):
            part = pl.ds(h * half + c * quarter, quarter)
            copies_a.append(
                pltpu.make_async_copy(a_hbm.at[part], a_v.at[part], sems.at[1 + 2 * c + h])
            )
            copies_a[-1].start()
    for c in range(Z_CUTS):
        part = pl.ds(c * slab, slab)
        copies_z.append(
            pltpu.make_async_copy(z_hbm.at[part], z_v.at[part], sems.at[1 + 2 * A_CUTS + c])
        )
        copies_z[-1].start()
    extra = split3(vec[...])
    for side in range(2):
        sent[side, pl.ds(count, PAD), :] = extra
    for c in range(A_CUTS):
        copies_a[2 * c].wait()
        copies_a[2 * c + 1].wait()
        for p in range(c * quarter, (c + 1) * quarter):
            pair = jnp.concatenate([a_v[p], a_v[p + half]], axis=0)
            x_v[pl.ds(p * pitch, nb), :] = pair.T.astype(F32)
    copy_idx.wait()
    for b in range(nb):
        if b * order % slab == 0:
            copies_z[b * order // slab].wait()
        at = b * order
        left = x_v[pl.ds(b, half, stride=pitch), :].astype(BF16)
        zb = z_v[pl.ds(at, order), :]
        zero = jnp.zeros_like(zb)
        right = jnp.concatenate(
            [jnp.concatenate([zb, zero], axis=1), jnp.concatenate([zero, zb], axis=1)], axis=0
        )
        out = jnp.dot(left, right, preferred_element_type=F32)
        w_v[pl.ds(at, order), :] = jnp.concatenate([out[:, :lanes], out[:, lanes:]], axis=0)
    mine = parity()
    leaving = []
    for slot, target in enumerate((cross, inner)):
        rows = rows_v.at[pl.ds(slot * count, count)]
        gather_rows(idx, mine if slot == 0 else 1 - mine, w_v, rows)
        sent[slot, pl.ds(0, count), :] = rows[...].astype(BF16)
        leaving.append(pltpu.make_async_copy(sent.at[slot], target, sems.at[slot]))
        leaving[-1].start()
    total = jnp.zeros((lanes, lanes), F32)
    for at in range(0, n, STEP):
        total += lax.dot_general(
            z_v[pl.ds(at, STEP), :],
            w_v[pl.ds(at, STEP), :].astype(BF16),
            (((0,), (0,)), ((), ())),
            preferred_element_type=F32,
        )
    self_v[...] = total
    leaving.append(pltpu.make_async_copy(self_v, self_block, sems.at[2]))
    leaving[-1].start()
    for copy in leaving:
        copy.wait()


def basis_kernel(idx, z, zt, z_f, rows_v):
    count = idx.shape[1]
    mine = parity()
    for at in range(0, z.shape[0], STEP):
        z_f[pl.ds(at, STEP), :] = z[pl.ds(at, STEP), :].astype(F32)
    for slot in range(2):
        rows = rows_v.at[pl.ds(slot * count, count)]
        gather_rows(idx, mine if slot == 0 else 1 - mine, z_f, rows)
    zt[...] = rows_v[...].astype(BF16).T


def pack_kernel(owner, cross, inner, zt, self_block, vec, tiles, product, row_v, used):
    lanes = self_block.shape[0]
    count = zt.shape[1] // 2
    mine = parity()

    def joined(ref):
        extra = ref[pl.ds(count, PAD), :].astype(F32)
        return extra[0:1] + (extra[1:2] + extra[2:3])

    tiles[...] = jnp.zeros_like(tiles)
    by_cross = jnp.dot(zt[:, :count], cross[pl.ds(0, count), :], preferred_element_type=F32)
    by_inner = jnp.dot(zt[:, count:], inner[pl.ds(0, count), :], preferred_element_type=F32)
    own = self_block[...]
    at = pl.multiple_of(mine * (2 * lanes), lanes)
    row_v[:, pl.ds(at, lanes)] = by_cross
    row_v[:, pl.ds(pl.multiple_of(2 * lanes - at, lanes), lanes)] = by_inner
    row_v[:, pl.ds(lanes, lanes)] = own
    total = by_cross * joined(cross) + own * vec[...] + by_inner * joined(inner)
    product[...] = jnp.sum(total.T, axis=0, keepdims=True)
    for q in range(tiles.shape[0]):
        used[q] = 0
    for t in range(owner.shape[1]):
        q = owner[0, t]
        slot = used[q]
        used[q] = slot + 1
        tiles[q, slot] = row_v[pl.ds(t * TR, TR), :]


def per_device(zbasis, stiff, ov_index, owner_map, coarse_vec):
    z = zbasis[0, 0]
    a = jnp.transpose(stiff[0, 0], (1, 2, 0))
    idx = ov_index[0, 0]
    owner = owner_map[0, 0, :, 0].reshape(1, -1)
    vec = coarse_vec[0]
    n, lanes = z.shape
    order, _, nb = a.shape
    count = idx.shape[1]
    chain = lax.axis_size("sub")
    owners = lax.axis_size("own")
    sent = jax.ShapeDtypeStruct((count + PAD, lanes), BF16)
    square = jax.ShapeDtypeStruct((lanes, lanes), F32)
    basis = jax.ShapeDtypeStruct((lanes, 2 * count), BF16)
    cross, inner, self_block = pl.pallas_call(
        apply_kernel,
        name="apply",
        out_shape=(sent, sent, square),
        in_specs=[HBM, HBM, HBM, VMEM],
        out_specs=(HBM, HBM, HBM),
        scratch_shapes=[
            pltpu.SMEM((2, count), jnp.int32),
            pltpu.VMEM((n, lanes), BF16),
            pltpu.VMEM((order, order, nb), BF16),
            pltpu.VMEM((order // 2 * (nb + 8), 2 * order), F32),
            pltpu.VMEM((n, lanes), F32),
            pltpu.VMEM((2 * count, lanes), F32),
            pltpu.VMEM((2, count + PAD, lanes), BF16),
            pltpu.VMEM((lanes, lanes), F32),
            pltpu.SemaphoreType.DMA((1 + 2 * A_CUTS + Z_CUTS,)),
        ],
        compiler_params=pltpu.CompilerParams(vmem_limit_bytes=ROOM),
        cost_estimate=pl.CostEstimate(flops=1 << 29, bytes_accessed=4 << 20, transcendentals=0),
    )(idx, z, a, vec)
    pairs = [(i, i + 1) for i in range(1, chain - 1, 2)]
    got_cross = lax.ppermute(cross, "sub", pairs + [(j, i) for i, j in pairs])
    got_inner = lax.ppermute(inner, "sub", [(i, i ^ 1) for i in range(chain)])
    zt = pl.pallas_call(
        basis_kernel,
        name="basis",
        out_shape=basis,
        in_specs=[SMEM, VMEM],
        out_specs=VMEM,
        scratch_shapes=[pltpu.VMEM((n, lanes), F32), pltpu.VMEM((2 * count, lanes), F32)],
        compiler_params=pltpu.CompilerParams(vmem_limit_bytes=BASIS_ROOM),
        cost_estimate=pl.CostEstimate(flops=1 << 28, bytes_accessed=2 << 20, transcendentals=0),
    )(idx, z)
    tiles, product = pl.pallas_call(
        pack_kernel,
        name="pack",
        out_shape=(
            jax.ShapeDtypeStruct((owners, SCAP, TR, 3 * lanes), F32),
            jax.ShapeDtypeStruct((1, lanes), F32),
        ),
        in_specs=[SMEM, VMEM, VMEM, VMEM, VMEM, VMEM],
        out_specs=(VMEM, VMEM),
        scratch_shapes=[pltpu.VMEM((lanes, 3 * lanes), F32), pltpu.SMEM((owners,), jnp.int32)],
        compiler_params=pltpu.CompilerParams(vmem_limit_bytes=PACK_ROOM),
    )(owner, got_cross, got_inner, zt, self_block, vec)
    received = lax.all_to_all(tiles, "own", 0, 0, tiled=True)
    return received[None, None], product[None]


def solution(mesh):
    in_specs = (
        P("sub", "own", None, None),
        P("sub", "own", None, None, None),
        P("sub", "own", None, None),
        P("sub", "own", None, None),
        P("sub", "own", None),
    )
    out_specs = (P("sub", "own", None, None, None, None), P("sub", "own", None))
    return jax.shard_map(
        per_device, mesh=mesh, in_specs=in_specs, out_specs=out_specs, check_vma=False
    )
```

```python
import jax
import jax.numpy as jnp
from jax import lax
from jax.experimental import pallas as pl
from jax.experimental.pallas import tpu as pltpu
from jax.sharding import PartitionSpec as P

TR = 8
SCAP = 8
PAD = 16
STEP = 1024
A_CUTS = 2
Z_CUTS = 2
ROOM = 58 << 20
BASIS_ROOM = 40 << 20
PACK_ROOM = 16 << 20
F32 = jnp.float32
BF16 = jnp.bfloat16
SMEM = pl.BlockSpec(memory_space=pltpu.SMEM)
VMEM = pl.BlockSpec(memory_space=pltpu.VMEM)
HBM = pl.BlockSpec(memory_space=pltpu.HBM)


def parity():
    return lax.rem(lax.axis_index("sub"), 2)


def split3(x):
    hi = x.astype(BF16)
    rest = x - hi.astype(F32)
    mid = rest.astype(BF16)
    low = (rest - mid.astype(F32)).astype(BF16)
    return jnp.concatenate([hi, mid, low, jnp.zeros((PAD - 3, x.shape[1]), BF16)], axis=0)


def gather_rows(idx, side, source, target):
    for r in range(idx.shape[1]):
        target[pl.ds(r, 1), :] = source[pl.ds(idx[side, r], 1), :]


def apply_kernel(
    idx_hbm, z_hbm, a_hbm, vec, cross, inner, self_block, z_v, idx, a_v, x_v, w_v, rows_v, sems
):
    order, _, nb = a_v.shape
    half = order // 2
    n, lanes = z_v.shape
    count = idx.shape[1]
    pitch = nb + 8
    quarter = half // A_CUTS
    slab = n // Z_CUTS
    copy_idx = pltpu.make_async_copy(idx_hbm, idx, sems.at[0])
    copy_idx.start()
    copies_a, copies_z = [], []
    for c in range(A_CUTS):
        for h in range(2):
            part = pl.ds(h * half + c * quarter, quarter)
            copies_a.append(
                pltpu.make_async_copy(a_hbm.at[part], a_v.at[part], sems.at[1 + 2 * c + h])
            )
            copies_a[-1].start()
    for c in range(Z_CUTS):
        part = pl.ds(c * slab, slab)
        copies_z.append(
            pltpu.make_async_copy(z_hbm.at[part], z_v.at[part], sems.at[1 + 2 * A_CUTS + c])
        )
        copies_z[-1].start()
    extra = split3(vec[...])
    for side in range(2):
        (cross, inner)[side][pl.ds(count, PAD), :] = extra
    for c in range(A_CUTS):
        copies_a[2 * c].wait()
        copies_a[2 * c + 1].wait()
        for p in range(c * quarter, (c + 1) * quarter):
            pair = jnp.concatenate([a_v[p], a_v[p + half]], axis=0)
            x_v[pl.ds(p * pitch, nb), :] = pair.T.astype(F32)
    copy_idx.wait()
    for b in range(nb):
        if b * order % slab == 0:
            copies_z[b * order // slab].wait()
        at = b * order
        left = x_v[pl.ds(b, half, stride=pitch), :].astype(BF16)
        zb = z_v[pl.ds(at, order), :]
        zero = jnp.zeros_like(zb)
        right = jnp.concatenate(
            [jnp.concatenate([zb, zero], axis=1), jnp.concatenate([zero, zb], axis=1)], axis=0
        )
        out = jnp.dot(left, right, preferred_element_type=F32)
        w_v[pl.ds(at, order), :] = jnp.concatenate([out[:, :lanes], out[:, lanes:]], axis=0)
    for side in range(2):
        gather_rows(idx, side, w_v, rows_v.at[pl.ds(side * count, count)])
    low, high = rows_v[pl.ds(0, count), :].astype(BF16), rows_v[pl.ds(count, count), :].astype(BF16)
    even = parity() == 0
    cross[pl.ds(0, count), :] = jnp.where(even, low, high)
    inner[pl.ds(0, count), :] = jnp.where(even, high, low)
    total = jnp.zeros((lanes, lanes), F32)
    for at in range(0, n, STEP):
        total += lax.dot_general(
            z_v[pl.ds(at, STEP), :],
            w_v[pl.ds(at, STEP), :].astype(BF16),
            (((0,), (0,)), ((), ())),
            preferred_element_type=F32,
        )
    self_block[...] = total


def basis_kernel(idx, z, zt, z_f, rows_v):
    count = idx.shape[1]
    for at in range(0, z.shape[0], STEP):
        z_f[pl.ds(at, STEP), :] = z[pl.ds(at, STEP), :].astype(F32)
    for slot in range(2):
        rows = rows_v.at[pl.ds(slot * count, count)]
        gather_rows(idx, slot, z_f, rows)
    zt[...] = rows_v[...].astype(BF16).T


def pack_kernel(owner, cross, inner, zt, self_block, vec, tiles, product, row_v, used):
    lanes = self_block.shape[0]
    count = zt.shape[1] // 2
    mine = parity()

    def joined(ref):
        extra = ref[pl.ds(count, PAD), :].astype(F32)
        return extra[0:1] + (extra[1:2] + extra[2:3])

    tiles[...] = jnp.zeros_like(tiles)
    near = pl.multiple_of(mine * count, count)
    far = pl.multiple_of((1 - mine) * count, count)
    by_cross = jnp.dot(zt[:, pl.ds(near, count)], cross[pl.ds(0, count), :], preferred_element_type=F32)
    by_inner = jnp.dot(zt[:, pl.ds(far, count)], inner[pl.ds(0, count), :], preferred_element_type=F32)
    own = self_block[...]
    at = pl.multiple_of(mine * (2 * lanes), lanes)
    row_v[:, pl.ds(at, lanes)] = by_cross
    row_v[:, pl.ds(pl.multiple_of(2 * lanes - at, lanes), lanes)] = by_inner
    row_v[:, pl.ds(lanes, lanes)] = own
    total = by_cross * joined(cross) + own * vec[...] + by_inner * joined(inner)
    product[...] = jnp.sum(total.T, axis=0, keepdims=True)
    for q in range(tiles.shape[0]):
        used[q] = 0
    for t in range(owner.shape[1]):
        q = owner[0, t]
        slot = used[q]
        used[q] = slot + 1
        tiles[q, slot] = row_v[pl.ds(t * TR, TR), :]


def per_device(zbasis, stiff, ov_index, owner_map, coarse_vec):
    z = zbasis[0, 0]
    a = jnp.transpose(stiff[0, 0], (1, 2, 0))
    idx = ov_index[0, 0]
    owner = owner_map[0, 0, :, 0].reshape(1, -1)
    vec = coarse_vec[0]
    n, lanes = z.shape
    order, _, nb = a.shape
    count = idx.shape[1]
    chain = lax.axis_size("sub")
    owners = lax.axis_size("own")
    sent = pltpu.VMEM((count + PAD, lanes), BF16)
    basis = jax.ShapeDtypeStruct((lanes, 2 * count), BF16)
    cross, inner, self_block, z = pl.pallas_call(
        apply_kernel,
        name="apply",
        out_shape=(sent, sent, pltpu.VMEM((lanes, lanes), F32), pltpu.VMEM((n, lanes), BF16)),
        in_specs=[HBM, HBM, HBM, VMEM],
        out_specs=(VMEM,) * 4,
        scratch_shapes=[
            pltpu.SMEM((2, count), jnp.int32),
            pltpu.VMEM((order, order, nb), BF16),
            pltpu.VMEM((order // 2 * (nb + 8), 2 * order), F32),
            pltpu.VMEM((n, lanes), F32),
            pltpu.VMEM((2 * count, lanes), F32),
            pltpu.SemaphoreType.DMA((1 + 2 * A_CUTS + Z_CUTS,)),
        ],
        compiler_params=pltpu.CompilerParams(vmem_limit_bytes=ROOM),
        cost_estimate=pl.CostEstimate(flops=1 << 29, bytes_accessed=4 << 20, transcendentals=0),
    )(idx, z, a, vec)
    pairs = [(i, i + 1) for i in range(1, chain - 1, 2)]
    got_cross = lax.ppermute(cross, "sub", pairs + [(j, i) for i, j in pairs])
    got_inner = lax.ppermute(inner, "sub", [(i, i ^ 1) for i in range(chain)])
    zt = pl.pallas_call(
        basis_kernel,
        name="basis",
        out_shape=basis,
        in_specs=[SMEM, VMEM],
        out_specs=VMEM,
        scratch_shapes=[pltpu.VMEM((n, lanes), F32), pltpu.VMEM((2 * count, lanes), F32)],
        compiler_params=pltpu.CompilerParams(vmem_limit_bytes=BASIS_ROOM),
        cost_estimate=pl.CostEstimate(flops=1 << 28, bytes_accessed=2 << 20, transcendentals=0),
    )(idx, z)
    tiles, product = pl.pallas_call(
        pack_kernel,
        name="pack",
        out_shape=(
            jax.ShapeDtypeStruct((owners, SCAP, TR, 3 * lanes), F32),
            jax.ShapeDtypeStruct((1, lanes), F32),
        ),
        in_specs=[SMEM, VMEM, VMEM, VMEM, VMEM, VMEM],
        out_specs=(VMEM, VMEM),
        scratch_shapes=[pltpu.VMEM((lanes, 3 * lanes), F32), pltpu.SMEM((owners,), jnp.int32)],
        compiler_params=pltpu.CompilerParams(vmem_limit_bytes=PACK_ROOM),
    )(owner, got_cross, got_inner, zt, self_block, vec)
    received = lax.all_to_all(tiles, "own", 0, 0, tiled=True)
    return received[None, None], product[None]


def solution(mesh):
    in_specs = (
        P("sub", "own", None, None),
        P("sub", "own", None, None, None),
        P("sub", "own", None, None),
        P("sub", "own", None, None),
        P("sub", "own", None),
    )
    out_specs = (P("sub", "own", None, None, None, None), P("sub", "own", None))
    return jax.shard_map(
        per_device, mesh=mesh, in_specs=in_specs, out_specs=out_specs, check_vma=False
    )
```

```python
import jax
import jax.numpy as jnp
from jax import lax
from jax.experimental import pallas as pl
from jax.experimental.pallas import tpu as pltpu
from jax.sharding import PartitionSpec as P

TR = 8
SCAP = 8
PAD = 16
STEP = 1024
LAP = 24
A_CUTS = 2
Z_CUTS = 2
ROOM = 58 << 20
BASIS_ROOM = 40 << 20
PACK_ROOM = 16 << 20
F32 = jnp.float32
BF16 = jnp.bfloat16
SMEM = pl.BlockSpec(memory_space=pltpu.SMEM)
VMEM = pl.BlockSpec(memory_space=pltpu.VMEM)
HBM = pl.BlockSpec(memory_space=pltpu.HBM)


def parity():
    return lax.rem(lax.axis_index("sub"), 2)


def early():
    return lax.rem(lax.axis_index("sub"), LAP) < 2


def split3(x):
    hi = x.astype(BF16)
    rest = x - hi.astype(F32)
    mid = rest.astype(BF16)
    low = (rest - mid.astype(F32)).astype(BF16)
    return jnp.concatenate([hi, mid, low, jnp.zeros((PAD - 3, x.shape[1]), BF16)], axis=0)


def gather_rows(idx, side, source, target):
    for r in range(idx.shape[1]):
        target[pl.ds(r, 1), :] = source[pl.ds(idx[side, r], 1), :]


def apply_kernel(
    idx_hbm, z_hbm, a_hbm, vec, cross, inner, self_block, z_v, zt, idx, a_v, x_v, w_v, rows_v, sems
):
    order, _, nb = a_v.shape
    half = order // 2
    n, lanes = z_v.shape
    count = idx.shape[1]
    pitch = nb + 8
    quarter = half // A_CUTS
    slab = n // Z_CUTS
    copy_idx = pltpu.make_async_copy(idx_hbm, idx, sems.at[0])
    copy_idx.start()
    copies_a, copies_z = [], []
    for c in range(A_CUTS):
        for h in range(2):
            part = pl.ds(h * half + c * quarter, quarter)
            copies_a.append(
                pltpu.make_async_copy(a_hbm.at[part], a_v.at[part], sems.at[1 + 2 * c + h])
            )
            copies_a[-1].start()
    for c in range(Z_CUTS):
        part = pl.ds(c * slab, slab)
        copies_z.append(
            pltpu.make_async_copy(z_hbm.at[part], z_v.at[part], sems.at[1 + 2 * A_CUTS + c])
        )
        copies_z[-1].start()
    extra = split3(vec[...])
    for side in range(2):
        (cross, inner)[side][pl.ds(count, PAD), :] = extra
    for c in range(A_CUTS):
        copies_a[2 * c].wait()
        copies_a[2 * c + 1].wait()
        for p in range(c * quarter, (c + 1) * quarter):
            pair = jnp.concatenate([a_v[p], a_v[p + half]], axis=0)
            x_v[pl.ds(p * pitch, nb), :] = pair.T.astype(F32)
    copy_idx.wait()
    for b in range(nb):
        if b * order % slab == 0:
            copies_z[b * order // slab].wait()
        at = b * order
        left = x_v[pl.ds(b, half, stride=pitch), :].astype(BF16)
        zb = z_v[pl.ds(at, order), :]
        zero = jnp.zeros_like(zb)
        right = jnp.concatenate(
            [jnp.concatenate([zb, zero], axis=1), jnp.concatenate([zero, zb], axis=1)], axis=0
        )
        out = jnp.dot(left, right, preferred_element_type=F32)
        w_v[pl.ds(at, order), :] = jnp.concatenate([out[:, :lanes], out[:, lanes:]], axis=0)
    for side in range(2):
        gather_rows(idx, side, w_v, rows_v.at[pl.ds(side * count, count)])
    low, high = rows_v[pl.ds(0, count), :].astype(BF16), rows_v[pl.ds(count, count), :].astype(BF16)
    even = parity() == 0
    cross[pl.ds(0, count), :] = jnp.where(even, low, high)
    inner[pl.ds(0, count), :] = jnp.where(even, high, low)
    total = jnp.zeros((lanes, lanes), F32)
    for at in range(0, n, STEP):
        total += lax.dot_general(
            z_v[pl.ds(at, STEP), :],
            w_v[pl.ds(at, STEP), :].astype(BF16),
            (((0,), (0,)), ((), ())),
            preferred_element_type=F32,
        )
    self_block[...] = total

    @pl.when(early())
    def _():
        basis_rows(idx, z_v, w_v, rows_v, zt)


def basis_rows(idx, z, z_f, rows_v, zt):
    count = idx.shape[1]
    for at in range(0, z.shape[0], STEP):
        z_f[pl.ds(at, STEP), :] = z[pl.ds(at, STEP), :].astype(F32)
    for side in range(2):
        gather_rows(idx, side, z_f, rows_v.at[pl.ds(side * count, count)])
    zt[...] = rows_v[...].astype(BF16).T


def basis_kernel(idx, z, given, zt, z_f, rows_v):
    ahead = early()

    @pl.when(ahead)
    def _():
        zt[...] = given[...]

    @pl.when(jnp.logical_not(ahead))
    def _():
        basis_rows(idx, z, z_f, rows_v, zt)


def pack_kernel(owner, cross, inner, zt, self_block, vec, tiles, product, row_v, used):
    lanes = self_block.shape[0]
    count = zt.shape[1] // 2
    mine = parity()

    def joined(ref):
        extra = ref[pl.ds(count, PAD), :].astype(F32)
        return extra[0:1] + (extra[1:2] + extra[2:3])

    tiles[...] = jnp.zeros_like(tiles)
    near = pl.multiple_of(mine * count, count)
    far = pl.multiple_of((1 - mine) * count, count)
    by_cross = jnp.dot(zt[:, pl.ds(near, count)], cross[pl.ds(0, count), :], preferred_element_type=F32)
    by_inner = jnp.dot(zt[:, pl.ds(far, count)], inner[pl.ds(0, count), :], preferred_element_type=F32)
    own = self_block[...]
    at = pl.multiple_of(mine * (2 * lanes), lanes)
    row_v[:, pl.ds(at, lanes)] = by_cross
    row_v[:, pl.ds(pl.multiple_of(2 * lanes - at, lanes), lanes)] = by_inner
    row_v[:, pl.ds(lanes, lanes)] = own
    total = by_cross * joined(cross) + own * vec[...] + by_inner * joined(inner)
    product[...] = jnp.sum(total.T, axis=0, keepdims=True)
    for q in range(tiles.shape[0]):
        used[q] = 0
    for t in range(owner.shape[1]):
        q = owner[0, t]
        slot = used[q]
        used[q] = slot + 1
        tiles[q, slot] = row_v[pl.ds(t * TR, TR), :]


def per_device(zbasis, stiff, ov_index, owner_map, coarse_vec):
    z = zbasis[0, 0]
    a = jnp.transpose(stiff[0, 0], (1, 2, 0))
    idx = ov_index[0, 0]
    owner = owner_map[0, 0, :, 0].reshape(1, -1)
    vec = coarse_vec[0]
    n, lanes = z.shape
    order, _, nb = a.shape
    count = idx.shape[1]
    chain = lax.axis_size("sub")
    owners = lax.axis_size("own")
    sent = pltpu.VMEM((count + PAD, lanes), BF16)
    basis = pltpu.VMEM((lanes, 2 * count), BF16)
    cross, inner, self_block, z, given = pl.pallas_call(
        apply_kernel,
        name="apply",
        out_shape=(sent, sent, pltpu.VMEM((lanes, lanes), F32), pltpu.VMEM((n, lanes), BF16), basis),
        in_specs=[HBM, HBM, HBM, VMEM],
        out_specs=(VMEM,) * 5,
        scratch_shapes=[
            pltpu.SMEM((2, count), jnp.int32),
            pltpu.VMEM((order, order, nb), BF16),
            pltpu.VMEM((order // 2 * (nb + 8), 2 * order), F32),
            pltpu.VMEM((n, lanes), F32),
            pltpu.VMEM((2 * count, lanes), F32),
            pltpu.SemaphoreType.DMA((1 + 2 * A_CUTS + Z_CUTS,)),
        ],
        compiler_params=pltpu.CompilerParams(vmem_limit_bytes=ROOM),
        cost_estimate=pl.CostEstimate(flops=1 << 29, bytes_accessed=4 << 20, transcendentals=0),
    )(idx, z, a, vec)
    pairs = [(i, i + 1) for i in range(1, chain - 1, 2)]
    got_cross = lax.ppermute(cross, "sub", pairs + [(j, i) for i, j in pairs])
    got_inner = lax.ppermute(inner, "sub", [(i, i ^ 1) for i in range(chain)])
    zt = pl.pallas_call(
        basis_kernel,
        name="basis",
        out_shape=basis,
        in_specs=[SMEM, VMEM, VMEM],
        out_specs=VMEM,
        scratch_shapes=[pltpu.VMEM((n, lanes), F32), pltpu.VMEM((2 * count, lanes), F32)],
        compiler_params=pltpu.CompilerParams(vmem_limit_bytes=BASIS_ROOM),
        cost_estimate=pl.CostEstimate(flops=1 << 28, bytes_accessed=2 << 20, transcendentals=0),
    )(idx, z, given)
    tiles, product = pl.pallas_call(
        pack_kernel,
        name="pack",
        out_shape=(
            jax.ShapeDtypeStruct((owners, SCAP, TR, 3 * lanes), F32),
            jax.ShapeDtypeStruct((1, lanes), F32),
        ),
        in_specs=[SMEM, VMEM, VMEM, VMEM, VMEM, VMEM],
        out_specs=(VMEM, VMEM),
        scratch_shapes=[pltpu.VMEM((lanes, 3 * lanes), F32), pltpu.SMEM((owners,), jnp.int32)],
        compiler_params=pltpu.CompilerParams(vmem_limit_bytes=PACK_ROOM),
    )(owner, got_cross, got_inner, zt, self_block, vec)
    received = lax.all_to_all(tiles, "own", 0, 0, tiled=True)
    return received[None, None], product[None]


def solution(mesh):
    in_specs = (
        P("sub", "own", None, None),
        P("sub", "own", None, None, None),
        P("sub", "own", None, None),
        P("sub", "own", None, None),
        P("sub", "own", None),
    )
    out_specs = (P("sub", "own", None, None, None, None), P("sub", "own", None))
    return jax.shard_map(
        per_device, mesh=mesh, in_specs=in_specs, out_specs=out_specs, check_vma=False
    )
```

```python
import jax
import jax.numpy as jnp
from jax import lax
from jax.experimental import pallas as pl
from jax.experimental.pallas import tpu as pltpu
from jax.sharding import PartitionSpec as P

TR = 8
SCAP = 8
PAD = 16
STEP = 1024
LAP = 24
A_CUTS = 2
Z_CUTS = 2
ROOM = 58 << 20
BASIS_ROOM = 40 << 20
PACK_ROOM = 16 << 20
F32 = jnp.float32
BF16 = jnp.bfloat16
SMEM = pl.BlockSpec(memory_space=pltpu.SMEM)
VMEM = pl.BlockSpec(memory_space=pltpu.VMEM)
HBM = pl.BlockSpec(memory_space=pltpu.HBM)


def parity():
    return lax.rem(lax.axis_index("sub"), 2)


def early():
    return lax.rem(lax.axis_index("sub"), LAP) < 2


def split3(x):
    hi = x.astype(BF16)
    rest = x - hi.astype(F32)
    mid = rest.astype(BF16)
    low = (rest - mid.astype(F32)).astype(BF16)
    return jnp.concatenate([hi, mid, low, jnp.zeros((PAD - 3, x.shape[1]), BF16)], axis=0)


def gather_rows(idx, side, source, target):
    for r in range(idx.shape[1]):
        target[pl.ds(r, 1), :] = source[pl.ds(idx[side, r], 1), :]


def apply_kernel(
    idx_hbm, z_hbm, a_hbm, vec, cross, inner, self_block, z_v, zt, applied, idx, a_v, x_v, w_v, rows_v, sems
):
    order, _, nb = a_v.shape
    half = order // 2
    n, lanes = z_v.shape
    count = idx.shape[1]
    pitch = nb + 8
    quarter = half // A_CUTS
    slab = n // Z_CUTS
    copy_idx = pltpu.make_async_copy(idx_hbm, idx, sems.at[0])
    copy_idx.start()
    copies_a, copies_z = [], []
    for c in range(A_CUTS):
        for h in range(2):
            part = pl.ds(h * half + c * quarter, quarter)
            copies_a.append(
                pltpu.make_async_copy(a_hbm.at[part], a_v.at[part], sems.at[1 + 2 * c + h])
            )
            copies_a[-1].start()
    for c in range(Z_CUTS):
        part = pl.ds(c * slab, slab)
        copies_z.append(
            pltpu.make_async_copy(z_hbm.at[part], z_v.at[part], sems.at[1 + 2 * A_CUTS + c])
        )
        copies_z[-1].start()
    extra = split3(vec[...])
    for side in range(2):
        (cross, inner)[side][pl.ds(count, PAD), :] = extra
    for c in range(A_CUTS):
        copies_a[2 * c].wait()
        copies_a[2 * c + 1].wait()
        for p in range(c * quarter, (c + 1) * quarter):
            pair = jnp.concatenate([a_v[p], a_v[p + half]], axis=0)
            x_v[pl.ds(p * pitch, nb), :] = pair.T.astype(F32)
    copy_idx.wait()
    for b in range(nb):
        if b * order % slab == 0:
            copies_z[b * order // slab].wait()
        at = b * order
        left = x_v[pl.ds(b, half, stride=pitch), :].astype(BF16)
        zb = z_v[pl.ds(at, order), :]
        zero = jnp.zeros_like(zb)
        right = jnp.concatenate(
            [jnp.concatenate([zb, zero], axis=1), jnp.concatenate([zero, zb], axis=1)], axis=0
        )
        out = jnp.dot(left, right, preferred_element_type=F32)
        out = jnp.concatenate([out[:, :lanes], out[:, lanes:]], axis=0)
        w_v[pl.ds(at, order), :] = out
        applied[pl.ds(at, order), :] = out.astype(BF16)
    for side in range(2):
        gather_rows(idx, side, w_v, rows_v.at[pl.ds(side * count, count)])
    low, high = rows_v[pl.ds(0, count), :].astype(BF16), rows_v[pl.ds(count, count), :].astype(BF16)
    even = parity() == 0
    cross[pl.ds(0, count), :] = jnp.where(even, low, high)
    inner[pl.ds(0, count), :] = jnp.where(even, high, low)

    @pl.when(early())
    def _():
        self_rows(z_v, applied, self_block)
        basis_rows(idx, z_v, w_v, rows_v, zt)


def self_rows(z, applied, self_block):
    total = jnp.zeros(self_block.shape, F32)
    for at in range(0, z.shape[0], STEP):
        total += lax.dot_general(
            z[pl.ds(at, STEP), :],
            applied[pl.ds(at, STEP), :],
            (((0,), (0,)), ((), ())),
            preferred_element_type=F32,
        )
    self_block[...] = total


def basis_rows(idx, z, z_f, rows_v, zt):
    count = idx.shape[1]
    for at in range(0, z.shape[0], STEP):
        z_f[pl.ds(at, STEP), :] = z[pl.ds(at, STEP), :].astype(F32)
    for side in range(2):
        gather_rows(idx, side, z_f, rows_v.at[pl.ds(side * count, count)])
    zt[...] = rows_v[...].astype(BF16).T


def basis_kernel(idx, z, applied, given, given_self, zt, self_block, z_f, rows_v):
    ahead = early()

    @pl.when(ahead)
    def _():
        zt[...] = given[...]
        self_block[...] = given_self[...]

    @pl.when(jnp.logical_not(ahead))
    def _():
        self_rows(z, applied, self_block)
        basis_rows(idx, z, z_f, rows_v, zt)


def pack_kernel(owner, cross, inner, zt, self_block, vec, tiles, product, row_v, used):
    lanes = self_block.shape[0]
    count = zt.shape[1] // 2
    mine = parity()

    def joined(ref):
        extra = ref[pl.ds(count, PAD), :].astype(F32)
        return extra[0:1] + (extra[1:2] + extra[2:3])

    tiles[...] = jnp.zeros_like(tiles)
    near = pl.multiple_of(mine * count, count)
    far = pl.multiple_of((1 - mine) * count, count)
    by_cross = jnp.dot(zt[:, pl.ds(near, count)], cross[pl.ds(0, count), :], preferred_element_type=F32)
    by_inner = jnp.dot(zt[:, pl.ds(far, count)], inner[pl.ds(0, count), :], preferred_element_type=F32)
    own = self_block[...]
    at = pl.multiple_of(mine * (2 * lanes), lanes)
    row_v[:, pl.ds(at, lanes)] = by_cross
    row_v[:, pl.ds(pl.multiple_of(2 * lanes - at, lanes), lanes)] = by_inner
    row_v[:, pl.ds(lanes, lanes)] = own
    total = by_cross * joined(cross) + own * vec[...] + by_inner * joined(inner)
    product[...] = jnp.sum(total.T, axis=0, keepdims=True)
    for q in range(tiles.shape[0]):
        used[q] = 0
    for t in range(owner.shape[1]):
        q = owner[0, t]
        slot = used[q]
        used[q] = slot + 1
        tiles[q, slot] = row_v[pl.ds(t * TR, TR), :]


def per_device(zbasis, stiff, ov_index, owner_map, coarse_vec):
    z = zbasis[0, 0]
    a = jnp.transpose(stiff[0, 0], (1, 2, 0))
    idx = ov_index[0, 0]
    owner = owner_map[0, 0, :, 0].reshape(1, -1)
    vec = coarse_vec[0]
    n, lanes = z.shape
    order, _, nb = a.shape
    count = idx.shape[1]
    chain = lax.axis_size("sub")
    owners = lax.axis_size("own")
    sent = pltpu.VMEM((count + PAD, lanes), BF16)
    square = pltpu.VMEM((lanes, lanes), F32)
    basis = pltpu.VMEM((lanes, 2 * count), BF16)
    cross, inner, given_self, z, given, applied = pl.pallas_call(
        apply_kernel,
        name="apply",
        out_shape=(sent, sent, square, pltpu.VMEM((n, lanes), BF16), basis, pltpu.VMEM((n, lanes), BF16)),
        in_specs=[HBM, HBM, HBM, VMEM],
        out_specs=(VMEM,) * 6,
        scratch_shapes=[
            pltpu.SMEM((2, count), jnp.int32),
            pltpu.VMEM((order, order, nb), BF16),
            pltpu.VMEM((order // 2 * (nb + 8), 2 * order), F32),
            pltpu.VMEM((n, lanes), F32),
            pltpu.VMEM((2 * count, lanes), F32),
            pltpu.SemaphoreType.DMA((1 + 2 * A_CUTS + Z_CUTS,)),
        ],
        compiler_params=pltpu.CompilerParams(vmem_limit_bytes=ROOM),
        cost_estimate=pl.CostEstimate(flops=1 << 29, bytes_accessed=4 << 20, transcendentals=0),
    )(idx, z, a, vec)
    pairs = [(i, i + 1) for i in range(1, chain - 1, 2)]
    got_cross = lax.ppermute(cross, "sub", pairs + [(j, i) for i, j in pairs])
    got_inner = lax.ppermute(inner, "sub", [(i, i ^ 1) for i in range(chain)])
    zt, self_block = pl.pallas_call(
        basis_kernel,
        name="basis",
        out_shape=(basis, square),
        in_specs=[SMEM] + [VMEM] * 4,
        out_specs=(VMEM, VMEM),
        scratch_shapes=[pltpu.VMEM((n, lanes), F32), pltpu.VMEM((2 * count, lanes), F32)],
        compiler_params=pltpu.CompilerParams(vmem_limit_bytes=BASIS_ROOM),
        cost_estimate=pl.CostEstimate(flops=1 << 28, bytes_accessed=2 << 20, transcendentals=0),
    )(idx, z, applied, given, given_self)
    tiles, product = pl.pallas_call(
        pack_kernel,
        name="pack",
        out_shape=(
            jax.ShapeDtypeStruct((owners, SCAP, TR, 3 * lanes), F32),
            jax.ShapeDtypeStruct((1, lanes), F32),
        ),
        in_specs=[SMEM, VMEM, VMEM, VMEM, VMEM, VMEM],
        out_specs=(VMEM, VMEM),
        scratch_shapes=[pltpu.VMEM((lanes, 3 * lanes), F32), pltpu.SMEM((owners,), jnp.int32)],
        compiler_params=pltpu.CompilerParams(vmem_limit_bytes=PACK_ROOM),
    )(owner, got_cross, got_inner, zt, self_block, vec)
    received = lax.all_to_all(tiles, "own", 0, 0, tiled=True)
    return received[None, None], product[None]


def solution(mesh):
    in_specs = (
        P("sub", "own", None, None),
        P("sub", "own", None, None, None),
        P("sub", "own", None, None),
        P("sub", "own", None, None),
        P("sub", "own", None),
    )
    out_specs = (P("sub", "own", None, None, None, None), P("sub", "own", None))
    return jax.shard_map(
        per_device, mesh=mesh, in_specs=in_specs, out_specs=out_specs, check_vma=False
    )
```

```python
import jax
import jax.numpy as jnp
from jax import lax
from jax.experimental import pallas as pl
from jax.experimental.pallas import tpu as pltpu
from jax.sharding import PartitionSpec as P

TR = 8
SCAP = 8
PAD = 16
STEP = 1024
LAP = 24
A_CUTS = 2
Z_CUTS = 2
ROOM = 58 << 20
BASIS_ROOM = 40 << 20
PACK_ROOM = 16 << 20
F32 = jnp.float32
BF16 = jnp.bfloat16
SMEM = pl.BlockSpec(memory_space=pltpu.SMEM)
VMEM = pl.BlockSpec(memory_space=pltpu.VMEM)
HBM = pl.BlockSpec(memory_space=pltpu.HBM)


def parity():
    return lax.rem(lax.axis_index("sub"), 2)


def early():
    return lax.rem(lax.axis_index("sub"), LAP) < 2


def split3(x):
    hi = x.astype(BF16)
    rest = x - hi.astype(F32)
    mid = rest.astype(BF16)
    low = (rest - mid.astype(F32)).astype(BF16)
    return jnp.concatenate([hi, mid, low, jnp.zeros((PAD - 3, x.shape[1]), BF16)], axis=0)


def gather_rows(idx, side, source, target):
    for r in range(idx.shape[1]):
        target[pl.ds(r, 1), :] = source[pl.ds(idx[side, r], 1), :]


def apply_kernel(
    idx_hbm, z_hbm, a_hbm, vec, cross, inner, self_block, z_v, zt, applied, idx, a_v, x_v, w_v, rows_v, sems
):
    order, _, nb = a_v.shape
    half = order // 2
    n, lanes = z_v.shape
    count = idx.shape[1]
    pitch = nb + 8
    quarter = half // A_CUTS
    slab = n // Z_CUTS
    copy_idx = pltpu.make_async_copy(idx_hbm, idx, sems.at[0])
    copy_idx.start()
    copies_a, copies_z = [], []
    for c in range(A_CUTS):
        for h in range(2):
            part = pl.ds(h * half + c * quarter, quarter)
            copies_a.append(
                pltpu.make_async_copy(a_hbm.at[part], a_v.at[part], sems.at[1 + 2 * c + h])
            )
            copies_a[-1].start()
    for c in range(Z_CUTS):
        part = pl.ds(c * slab, slab)
        copies_z.append(
            pltpu.make_async_copy(z_hbm.at[part], z_v.at[part], sems.at[1 + 2 * A_CUTS + c])
        )
        copies_z[-1].start()
    extra = split3(vec[...])
    for side in range(2):
        (cross, inner)[side][pl.ds(count, PAD), :] = extra
    for c in range(A_CUTS):
        copies_a[2 * c].wait()
        copies_a[2 * c + 1].wait()
        for p in range(c * quarter, (c + 1) * quarter):
            pair = jnp.concatenate([a_v[p], a_v[p + half]], axis=0)
            x_v[pl.ds(p * pitch, nb), :] = pair.T.astype(F32)
    copy_idx.wait()
    for b in range(nb):
        if b * order % slab == 0:
            copies_z[b * order // slab].wait()
        at = b * order
        left = x_v[pl.ds(b, half, stride=pitch), :].astype(BF16)
        zb = z_v[pl.ds(at, order), :]
        zero = jnp.zeros_like(zb)
        right = jnp.concatenate(
            [jnp.concatenate([zb, zero], axis=1), jnp.concatenate([zero, zb], axis=1)], axis=0
        )
        out = jnp.dot(left, right, preferred_element_type=F32)
        out = jnp.concatenate([out[:, :lanes], out[:, lanes:]], axis=0)
        w_v[pl.ds(at, order), :] = out
        applied[pl.ds(at, order), :] = out.astype(BF16)
    for side in range(2):
        gather_rows(idx, side, w_v, rows_v.at[pl.ds(side * count, count)])
    low, high = rows_v[pl.ds(0, count), :].astype(BF16), rows_v[pl.ds(count, count), :].astype(BF16)
    even = parity() == 0
    cross[pl.ds(0, count), :] = jnp.where(even, low, high)
    inner[pl.ds(0, count), :] = jnp.where(even, high, low)

    @pl.when(early())
    def _():
        self_rows(z_v, applied, self_block)
        basis_rows(idx, z_v, w_v, rows_v, zt)


def self_rows(z, applied, self_block):
    total = jnp.zeros(self_block.shape, F32)
    for at in range(0, z.shape[0], STEP):
        total += lax.dot_general(
            z[pl.ds(at, STEP), :],
            applied[pl.ds(at, STEP), :],
            (((0,), (0,)), ((), ())),
            preferred_element_type=F32,
        )
    self_block[...] = total


def basis_rows(idx, z, z_f, rows_v, zt):
    count = idx.shape[1]
    for at in range(0, z.shape[0], STEP):
        z_f[pl.ds(at, STEP), :] = z[pl.ds(at, STEP), :].astype(F32)
    for side in range(2):
        gather_rows(idx, side, z_f, rows_v.at[pl.ds(side * count, count)])
    zt[...] = rows_v[...].astype(BF16).T


def basis_kernel(idx, z, applied, given, given_self, zt, self_block, z_f, rows_v):
    ahead = early()

    @pl.when(ahead)
    def _():
        zt[...] = given[...]
        self_block[...] = given_self[...]

    @pl.when(jnp.logical_not(ahead))
    def _():
        self_rows(z, applied, self_block)
        basis_rows(idx, z, z_f, rows_v, zt)


def pack_kernel(owner, cross, inner, zt, self_block, vec, tiles, product, row_v, used):
    lanes = self_block.shape[0]
    count = zt.shape[1] // 2
    mine = parity()

    def joined(ref):
        extra = ref[pl.ds(count, PAD), :].astype(F32)
        return extra[0:1] + (extra[1:2] + extra[2:3])

    tiles[...] = jnp.zeros_like(tiles)
    near = pl.multiple_of(mine * count, count)
    far = pl.multiple_of((1 - mine) * count, count)
    by_cross = jnp.dot(zt[:, pl.ds(near, count)], cross[pl.ds(0, count), :], preferred_element_type=F32)
    by_inner = jnp.dot(zt[:, pl.ds(far, count)], inner[pl.ds(0, count), :], preferred_element_type=F32)
    own = self_block[...]
    at = pl.multiple_of(mine * (2 * lanes), lanes)
    row_v[:, pl.ds(at, lanes)] = by_cross
    row_v[:, pl.ds(pl.multiple_of(2 * lanes - at, lanes), lanes)] = by_inner
    row_v[:, pl.ds(lanes, lanes)] = own
    total = by_cross * joined(cross) + own * vec[...] + by_inner * joined(inner)
    product[...] = jnp.sum(total, axis=1).reshape(1, -1)
    for q in range(tiles.shape[0]):
        used[q] = 0
    for t in range(owner.shape[1]):
        q = owner[0, t]
        slot = used[q]
        used[q] = slot + 1
        tiles[q, slot] = row_v[pl.ds(t * TR, TR), :]


def per_device(zbasis, stiff, ov_index, owner_map, coarse_vec):
    z = zbasis[0, 0]
    a = jnp.transpose(stiff[0, 0], (1, 2, 0))
    idx = ov_index[0, 0]
    owner = owner_map[0, 0, :, 0].reshape(1, -1)
    vec = coarse_vec[0]
    n, lanes = z.shape
    order, _, nb = a.shape
    count = idx.shape[1]
    chain = lax.axis_size("sub")
    owners = lax.axis_size("own")
    sent = pltpu.VMEM((count + PAD, lanes), BF16)
    square = pltpu.VMEM((lanes, lanes), F32)
    basis = pltpu.VMEM((lanes, 2 * count), BF16)
    cross, inner, given_self, z, given, applied = pl.pallas_call(
        apply_kernel,
        name="apply",
        out_shape=(sent, sent, square, pltpu.VMEM((n, lanes), BF16), basis, pltpu.VMEM((n, lanes), BF16)),
        in_specs=[HBM, HBM, HBM, VMEM],
        out_specs=(VMEM,) * 6,
        scratch_shapes=[
            pltpu.SMEM((2, count), jnp.int32),
            pltpu.VMEM((order, order, nb), BF16),
            pltpu.VMEM((order // 2 * (nb + 8), 2 * order), F32),
            pltpu.VMEM((n, lanes), F32),
            pltpu.VMEM((2 * count, lanes), F32),
            pltpu.SemaphoreType.DMA((1 + 2 * A_CUTS + Z_CUTS,)),
        ],
        compiler_params=pltpu.CompilerParams(vmem_limit_bytes=ROOM),
        cost_estimate=pl.CostEstimate(flops=1 << 29, bytes_accessed=4 << 20, transcendentals=0),
    )(idx, z, a, vec)
    pairs = [(i, i + 1) for i in range(1, chain - 1, 2)]
    got_cross = lax.ppermute(cross, "sub", pairs + [(j, i) for i, j in pairs])
    got_inner = lax.ppermute(inner, "sub", [(i, i ^ 1) for i in range(chain)])
    zt, self_block = pl.pallas_call(
        basis_kernel,
        name="basis",
        out_shape=(basis, square),
        in_specs=[SMEM] + [VMEM] * 4,
        out_specs=(VMEM, VMEM),
        scratch_shapes=[pltpu.VMEM((n, lanes), F32), pltpu.VMEM((2 * count, lanes), F32)],
        compiler_params=pltpu.CompilerParams(vmem_limit_bytes=BASIS_ROOM),
        cost_estimate=pl.CostEstimate(flops=1 << 28, bytes_accessed=2 << 20, transcendentals=0),
    )(idx, z, applied, given, given_self)
    tiles, product = pl.pallas_call(
        pack_kernel,
        name="pack",
        out_shape=(
            jax.ShapeDtypeStruct((owners, SCAP, TR, 3 * lanes), F32),
            jax.ShapeDtypeStruct((1, lanes), F32),
        ),
        in_specs=[SMEM, VMEM, VMEM, VMEM, VMEM, VMEM],
        out_specs=(VMEM, VMEM),
        scratch_shapes=[pltpu.VMEM((lanes, 3 * lanes), F32), pltpu.SMEM((owners,), jnp.int32)],
        compiler_params=pltpu.CompilerParams(vmem_limit_bytes=PACK_ROOM),
    )(owner, got_cross, got_inner, zt, self_block, vec)
    received = lax.all_to_all(tiles, "own", 0, 0, tiled=True)
    return received[None, None], product[None]


def solution(mesh):
    in_specs = (
        P("sub", "own", None, None),
        P("sub", "own", None, None, None),
        P("sub", "own", None, None),
        P("sub", "own", None, None),
        P("sub", "own", None),
    )
    out_specs = (P("sub", "own", None, None, None, None), P("sub", "own", None))
    return jax.shard_map(
        per_device, mesh=mesh, in_specs=in_specs, out_specs=out_specs, check_vma=False
    )
```
